512 devices in a mesh: section: 32 (over y_lo, x, core), tp: 16 (over y_hi, z).
Axes of the slice: x: 4, y: 8 (y_hi: 2, y_lo: 4; y = y_hi * 4 + y_lo), z: 8, core: 2. Of those that a mesh axis runs over, the one named last changes fastest.
Arguments:
- image_feats: bfloat16 [2, 128, 7680], P(None, 'section', 'tp'), may hold values from -6 to 6
- kv_weight: bfloat16 [32, 7680, 1024], P('section', 'tp'), may hold values from -0.0625 to 0.0625
- queries: bfloat16 [32, 2, 64, 8192], P('section', None, None, 'tp'), may hold values from -6 to 6
- query_gain: float32 [16, 128], replicated, may hold values from 0.25 to 1.75
- key_gain: float32 [16, 128], replicated, may hold values from 0.25 to 1.75
- gate_logit: float32 [16], replicated, may hold values from 0.3 to 1.5
- cotangent: bfloat16 [32, 2, 64, 8192], P('section', None, None, 'tp'), may hold values from -6 to 6
Outputs:
- residual_sum: bfloat16 [32, 2, 64, 8192], P('section', None, None, 'tp')
- query_grad: bfloat16 [32, 2, 64, 8192], P('section', None, None, 'tp')
- weight_grad: bfloat16 [32, 7680, 1024], P('section', 'tp')
- image_grad: float32 [2, 128, 7680], P(None, 'section', 'tp')
- gate_grad: float32 [16], replicated
The draws below stay inside these ranges and needn't reach their ends.
All inputs are finite; a program needn't handle non-finite values.
Results may differ from the reference program's by a relative error of at most 0.033.
Values may be sent and summed in bfloat16 or wider, within the bound.
No kernel may reach another device: no remote copies, remote signals or barrier semaphores. Data moves between devices by JAX's collectives and lax.ppermute only.
A program may use at most 128 MiB of HBM per device.

```python
import math
import jax
import jax.numpy as jnp
from jax import lax

D = 8192
HEADS = 64
KVH = 8
HD = 128
V = 7680
MB = 2
TOKH = 64
IMG = 128
SECTIONS = 16
KVW = 2048


def block_levels(key, extent, pieces, low, top_value):
    def one(axis_at, shards_of):
        draws = jax.random.uniform(jax.random.fold_in(jax.random.fold_in(key, 6), axis_at), (shards_of,), jnp.float32, low / len(pieces), top_value / len(pieces))
        return jnp.repeat(jnp.exp(draws), extent[axis_at] // shards_of).reshape((-1,) + (1,) * (len(extent) - axis_at - 1))

    factor_of = one(*pieces[0])
    for cut in pieces[1:]:
        factor_of = factor_of * one(*cut)
    return factor_of


def bell_draw(own_key, dims, width, limit, pieces=(), held_as=jnp.bfloat16):
    level = block_levels(own_key, dims, pieces, -0.22, 0.18) if pieces else 1.0
    entries = jax.random.normal(own_key, dims, jnp.float32) * width * level
    return jnp.minimum(jnp.maximum(entries, -limit), limit).astype(held_as)


def setup_inputs(seed: int = 0) -> dict:
    splits = jax.random.split(jax.random.key(seed), 8)
    image_feats = bell_draw(splits[0], (MB, IMG, V), 1.0, 6.0, ((1, 32), (2, 16)))
    kv_weight = bell_draw(splits[1], (2 * SECTIONS, V, KVW // 2), V ** -0.5, 0.0625, ((0, 32), (1, 16)))
    queries = bell_draw(splits[2], (2 * SECTIONS, MB, TOKH, D), 1.0, 6.0, ((0, 32), (3, 16)))
    query_gain = jnp.clip(1.0 + 0.15 * jax.random.normal(splits[3], (SECTIONS, HD), jnp.float32), 0.25, 1.75)
    key_gain = jnp.clip(1.0 + 0.15 * jax.random.normal(splits[4], (SECTIONS, HD), jnp.float32), 0.25, 1.75)
    gate_logit = jnp.clip(jax.random.uniform(splits[5], (SECTIONS,), jnp.float32, 0.3, 1.5), 0.3, 1.5)
    cotangent = bell_draw(splits[6], (2 * SECTIONS, MB, TOKH, D), 1.0, 6.0, ((0, 32), (3, 16)))
    return dict(image_feats=image_feats, kv_weight=kv_weight, queries=queries, query_gain=query_gain, key_gain=key_gain, gate_logit=gate_logit, cotangent=cotangent)


EPS = 1e-05

def rms_norm(values, gain):
    inverse = lax.rsqrt(lax.optimization_barrier(jnp.mean(values * values, axis=-1, keepdims=True)) + EPS)
    return (values * inverse * gain, inverse)

def norm_back(values, inverse, gain, upstream):
    weighted = gain * upstream
    inner = lax.optimization_barrier(jnp.mean(values * weighted, axis=-1, keepdims=True))
    return inverse * (weighted - values * inverse * inverse * inner)

def reference(image_feats, kv_weight, queries, query_gain, key_gain, gate_logit, cotangent):
    f32 = jnp.float32
    bf16 = jnp.bfloat16
    group_size = HEADS // KVH
    scale = 1.0 / math.sqrt(HD)
    half_width = KVW // 2
    tok_all = 2 * TOKH
    weights = kv_weight.reshape(SECTIONS, 2, V, half_width).transpose(0, 2, 1, 3).reshape(SECTIONS, V, KVW)

    def to_layers(values):
        return values.reshape(SECTIONS, 2, MB, TOKH, D).transpose(0, 2, 1, 3, 4).reshape(SECTIONS, MB, tok_all, D)

    def from_layers(values):
        return values.reshape(SECTIONS, MB, 2, TOKH, D).transpose(0, 2, 1, 3, 4).reshape(2 * SECTIONS, MB, TOKH, D)
    flat_image = image_feats.reshape(MB * IMG, V)
    layer_queries = to_layers(queries)
    cot_all = to_layers(cotangent).astype(f32)
    upstream_all = jnp.flip(jnp.cumsum(jnp.flip(cot_all, 0), 0), 0)

    def one_section(carry, inputs):
        weight, query_block, q_gain, k_gain, logit, upstream = inputs
        kv_values = jnp.dot(flat_image, weight, preferred_element_type=f32).astype(bf16)
        kv_five = kv_values.reshape(MB, IMG, KVH, 2, HD)
        key_rows = kv_five[:, :, :, 0, :].astype(f32)
        value_rows = kv_five[:, :, :, 1, :].astype(f32)
        key_hat, key_inverse = rms_norm(key_rows, k_gain)
        key_low = key_hat.astype(bf16).astype(f32)
        query_rows = query_block.reshape(MB, tok_all, KVH, group_size, HD).astype(f32)
        query_hat, query_inverse = rms_norm(query_rows, q_gain)
        query_low = query_hat.astype(bf16).astype(f32)
        scores = jnp.einsum('mtkge,mike->mkgti', query_low, key_low) * scale
        peak = lax.optimization_barrier(jnp.max(scores, axis=-1, keepdims=True))
        expo = jnp.exp(scores - peak)
        probs = expo / lax.optimization_barrier(jnp.sum(expo, axis=-1, keepdims=True))
        probs_low = probs.astype(bf16).astype(f32)
        attn = jnp.einsum('mkgti,mike->mtkge', probs_low, value_rows)
        gate_tanh = jnp.tanh(logit)
        branch = (gate_tanh * attn).astype(bf16).reshape(MB, tok_all, D)
        upstream_heads = upstream.reshape(MB, tok_all, KVH, group_size, HD)
        gate_grad = (1.0 - gate_tanh * gate_tanh) * jnp.sum(upstream_heads * attn)
        d_attn = (gate_tanh * upstream_heads).astype(bf16).astype(f32)
        d_prob = jnp.einsum('mtkge,mike->mkgti', d_attn, value_rows)
        d_score = probs * (d_prob - lax.optimization_barrier(jnp.sum(d_prob * probs, axis=-1, keepdims=True))) * scale
        d_score = d_score.astype(bf16).astype(f32)
        d_value = jnp.einsum('mkgti,mtkge->mike', probs_low, d_attn)
        d_key_hat = jnp.einsum('mkgti,mtkge->mike', d_score, query_low)
        d_query_hat = jnp.einsum('mkgti,mike->mtkge', d_score, key_low)
        d_keys = norm_back(key_rows, key_inverse, k_gain, d_key_hat).astype(bf16)
        d_kv = jnp.stack([d_keys, d_value.astype(bf16)], axis=3).reshape(MB * IMG, KVW)
        query_grad = norm_back(query_rows, query_inverse, q_gain, d_query_hat).astype(bf16).reshape(MB, tok_all, D)
        weight_grad = jnp.dot(flat_image.T, d_kv, preferred_element_type=f32).astype(bf16)
        image_term = jnp.dot(d_kv, weight.T, preferred_element_type=f32)
        return (carry + image_term, (branch, query_grad, weight_grad, gate_grad))
    start = jnp.zeros((MB * IMG, V), f32)
    image_total, outputs = lax.scan(one_section, start, (weights, layer_queries, query_gain, key_gain, gate_logit, upstream_all))
    branches, query_grads, weight_grads, gate_grads = outputs
    residual_sum = jnp.cumsum(branches.astype(f32), 0).astype(bf16)
    weight_out = weight_grads.reshape(SECTIONS, V, 2, half_width).transpose(0, 2, 1, 3).reshape(2 * SECTIONS, V, half_width)
    return (from_layers(residual_sum), from_layers(query_grads), weight_out, image_total.reshape(MB, IMG, V), gate_grads)
```

```python
import math

import jax
import jax.numpy as jnp
from jax import lax
from jax.experimental import pallas as pl
from jax.experimental.pallas import tpu as pltpu
from jax.sharding import Mesh, PartitionSpec as P

F32 = jnp.float32
BF16 = jnp.bfloat16
EPS = 1e-05
HD = 128
FEAT = 480
WIDE = 512
ROWS = 128
TILE = 8
LAYERS = 16
TP = 16
SCALE = 1.0 / math.sqrt(HD)
MASKED = -1e30

SECTION = ("yl", "x", "core")
LAYER = ("yl", "x")
TPAX = ("yh", "zh", "zl")
QUAD = ("core", "zl")

NT = (((1,), (1,)), ((), ()))
TN = (((0,), (0,)), ((), ()))


def call(body, outs, *args, smem=(), scratch=()):
    specs = [
        pl.BlockSpec(memory_space=pltpu.SMEM if i in smem else pltpu.VMEM) for i in range(len(args))
    ]
    vmem = pl.BlockSpec(memory_space=pltpu.VMEM)
    return pl.pallas_call(
        body,
        out_shape=[jax.ShapeDtypeStruct(*o) for o in outs],
        in_specs=specs,
        out_specs=[vmem] * len(outs),
        scratch_shapes=list(scratch),
        compiler_params=pltpu.CompilerParams(vmem_limit_bytes=40 * 2**20),
    )(*args)


def dot(a, b, dims=(((1,), (0,)), ((), ()))):
    return lax.dot_general(a, b, dims, preferred_element_type=F32)


def stack_heads(x):
    return jnp.concatenate([x[:, h * HD : (h + 1) * HD] for h in range(4)], axis=0)


def unstack_heads(x):
    return jnp.concatenate([x[h * ROWS : (h + 1) * ROWS] for h in range(4)], axis=1)


def pick_row(ref, layer):
    return ref[pl.ds(layer, 1), :]


def three_parts(x):
    first = x.astype(BF16).astype(F32)
    second = (x - first).astype(BF16).astype(F32)
    third = x - first - second
    lane = lax.broadcasted_iota(jnp.int32, (16, HD), 1)
    row = lax.broadcasted_iota(jnp.int32, (16, HD), 0)
    tile = jnp.where(lane == 0, first, jnp.where(lane == 1, second, jnp.where(lane == 2, third, 0.0)))
    return jnp.where(row == 0, tile, 0.0)


def pack_body(img, cot, out, wide):
    wide[...] = jnp.zeros((TILE, WIDE), F32)
    wide[0:4, 0:FEAT] = img[0].astype(F32)
    wide[4:8, 0:FEAT] = img[1].astype(F32)
    rows = wide[...]
    for m in range(2):
        part = cot[0, m].astype(F32)
        for i in range(8):
            both = jnp.concatenate([rows, part[i * TILE : (i + 1) * TILE]], axis=0)
            out[m * 8 + i] = both.astype(BF16)


def project_body(ids, gathered, w_own, w_oth, partials, image, upstream):
    core = ids[1]
    every = gathered[...].astype(F32)
    rows = every[:, :TILE].reshape(ROWS, WIDE).astype(BF16)
    image[...] = rows
    feats = rows[:, :FEAT]
    for which, w in ((0, w_own), (1, w_oth)):
        half = core if which == 0 else 1 - core
        sums = dot(feats, w[0]).astype(BF16)
        for k in range(4):
            for z in range(2):
                partials[8 * half + 2 * k + z] = sums[z * 64 : (z + 1) * 64, k * 256 : (k + 1) * 256]
    total = jnp.zeros((TILE, WIDE), F32)
    for j in reversed(range(LAYERS)):
        total = total + every[j, TILE:]
        upstream[j] = total


def sum_body(pieces, out):
    total = pieces[0].astype(F32)
    for t in range(1, TP):
        total = total + pieces[t].astype(F32)
    total = total.astype(BF16)
    for q in range(4):
        out[q] = total


def norm(x):
    return lax.rsqrt(jnp.mean(x * x, axis=-1, keepdims=True) + EPS)


def gate_of(gate, layer):
    return jnp.tanh(jnp.full((1, 1), gate[layer], F32))


def forward_body(ids, gate, kv, queries, query_gain, key_gain, upstream, out, probs_out, attn_out):
    layer = ids[0]
    both = kv[...].reshape(256, 256)
    keys = both[:, :HD].astype(F32)
    key_low = (keys * norm(keys) * pick_row(key_gain, layer)).astype(BF16)
    rows = stack_heads(queries[0].reshape(ROWS, WIDE)).astype(F32)
    query_low = (rows * norm(rows) * pick_row(query_gain, layer)).astype(BF16)
    scores = dot(query_low, key_low, NT) * SCALE
    of_query = (lax.broadcasted_iota(jnp.int32, scores.shape, 0) >> 6) & 1
    of_key = (lax.broadcasted_iota(jnp.int32, scores.shape, 1) >> 2) & 1
    scores = jnp.where(of_query == of_key, scores, MASKED)
    expo = jnp.exp(scores - jnp.max(scores, axis=-1, keepdims=True))
    probs = expo / jnp.sum(expo, axis=-1, keepdims=True)
    probs_out[...] = probs
    attn = dot(probs.astype(BF16), both[:, HD:])
    attn_out[...] = attn
    branch = unstack_heads((gate_of(gate, layer) * attn)).reshape(LAYERS, TILE, WIDE)
    out[...] = jnp.concatenate([upstream[...], branch], axis=1).astype(BF16)


def norm_back(values, inverse, gain, upstream):
    weighted = gain * upstream
    inner = jnp.mean(values * weighted, axis=-1, keepdims=True)
    return inverse * (weighted - values * inverse * inverse * inner)


def backward_body(
    ids, gate, mid, kv, queries, query_gain, key_gain, probs_in, attn_in, out, query_grad
):
    layer = ids[0]
    both = kv[...].reshape(256, 256)
    keys = both[:, :HD].astype(F32)
    key_low = (keys * norm(keys) * pick_row(key_gain, layer)).astype(BF16)
    rows = stack_heads(queries[0].reshape(ROWS, WIDE)).astype(F32)
    inverse = norm(rows)
    gain = pick_row(query_gain, layer)
    query_low = (rows * inverse * gain).astype(BF16)
    probs = probs_in[...]
    upstream = stack_heads(mid[...].astype(F32)[:, :TILE].reshape(ROWS, WIDE))
    tanh = gate_of(gate, layer)
    by_row = jnp.sum(upstream * attn_in[...], axis=1, keepdims=True)
    gate_sum = (1.0 - tanh * tanh) * jnp.sum(by_row, axis=0, keepdims=True)
    d_attn = (tanh * upstream).astype(BF16)
    d_prob = dot(d_attn, both[:, HD:], NT)
    inner = jnp.sum(d_prob * probs, axis=-1, keepdims=True)
    d_score = (probs * (d_prob - inner) * SCALE).astype(BF16)
    d_value = dot(probs.astype(BF16), d_attn, TN)
    d_key_hat = dot(d_score, query_low, TN)
    d_query_hat = dot(d_score, key_low)
    grad = unstack_heads(norm_back(rows, inverse, gain, d_query_hat))
    query_grad[...] = grad.astype(BF16).reshape(1, 2, 64, WIDE)
    extra = three_parts(gate_sum).astype(BF16)
    for q in range(4):
        out[q, 0:64] = d_key_hat[q * 64 : (q + 1) * 64].astype(BF16)
        out[q, 64:128] = d_value[q * 64 : (q + 1) * 64].astype(BF16)
        out[q, 128:144] = extra


def grad_body(ids, pieces, kv_own, key_gain, out):
    total = pieces[0].astype(F32)
    for q in range(1, 4):
        total = total + pieces[q].astype(F32)
    keys = kv_own[0][:, :HD].astype(F32)
    d_keys = norm_back(keys, norm(keys), pick_row(key_gain, ids[0]), total[0:64])
    gate_sum = jnp.sum(total[128:136], axis=1, keepdims=True)[0:1]
    extra = three_parts(gate_sum)
    tile = jnp.concatenate([d_keys, total[64:128], extra], axis=0).astype(BF16)
    for t in range(TP):
        out[t] = tile


def columns(pieces, half):
    parts = []
    for z in range(2):
        row = []
        for k in range(4):
            tile = pieces[8 * half + 2 * k + z]
            row += [tile[0:64], tile[64:128]]
        parts.append(jnp.concatenate(row, axis=1))
    return jnp.concatenate(parts, axis=0)


def image_body(ids, pieces, w_own, w_oth, mid, out, own_grads, oth_grads, wide):
    core = ids[1]
    own = columns(pieces, core)
    oth = columns(pieces, 1 - core)
    own_grads[...] = own
    oth_grads[...] = oth
    term = dot(own, w_own[0], NT) + dot(oth, w_oth[0], NT)
    gate_rows = pieces[0][128:144].astype(F32)[0:TILE]
    for t in range(1, TP):
        gate_rows = gate_rows + pieces[t][128:144].astype(F32)[0:TILE]
    gate_sum = 0.5 * jnp.sum(gate_rows, axis=1, keepdims=True)[0:1]
    wide[:, WIDE - HD :] = jnp.zeros((ROWS, HD), F32)
    wide[:, 0:FEAT] = term
    tile = three_parts(gate_sum)[0:1]
    tail = jnp.broadcast_to(tile[:, 0:3], (ROWS, 3))
    wide[:, FEAT : FEAT + 3] = tail
    image = wide[...].reshape(LAYERS, TILE, WIDE)
    total = jnp.zeros((TILE, WIDE), F32)
    for i in range(LAYERS):
        total = total + mid[i].astype(F32)[TILE:]
        out[i] = jnp.concatenate([image[i], total], axis=0).astype(BF16)


def weight_body(image_own, image_oth, own_grads, oth_grads, out):
    total = dot(image_own[:, :FEAT], own_grads[...], TN)
    total = total + dot(image_oth[:, :FEAT], oth_grads[...], TN)
    out[0] = total.astype(BF16)


def final_body(returned, residual, image, gates):
    total = jnp.zeros((TILE, WIDE), F32)
    lane = lax.broadcasted_iota(jnp.int32, (1, HD), 1)
    line = jnp.zeros((1, HD), F32)
    for i in range(LAYERS):
        both = returned[i].astype(F32)
        total = total + both[:TILE]
        tail = jnp.sum(both[0:1, FEAT : FEAT + 3], axis=1, keepdims=True)
        line = line + jnp.where(lane == i, tail, 0.0)
        m, at = divmod(i * TILE, 64)
        residual[0, m, at : at + TILE] = both[TILE:].astype(BF16)
    image[0] = total[0:4, :FEAT]
    image[1] = total[4:8, :FEAT]
    gates[...] = line[:, :LAYERS]


def swap_cores(x):
    return lax.ppermute(x, "core", [(0, 1), (1, 0)])


def exchange(x, axes):
    return lax.all_to_all(x, axes, 0, 0)


def local(image_feats, kv_weight, queries, query_gain, key_gain, gate_logit, cotangent):
    layer = lax.axis_index(LAYER)
    ids = jnp.stack([layer, lax.axis_index("core")]).astype(jnp.int32)
    other_weight = swap_cores(kv_weight)
    (packed,) = call(
        pack_body,
        [((LAYERS, 16, WIDE), BF16)],
        image_feats,
        cotangent,
        scratch=[pltpu.VMEM((TILE, WIDE), F32)],
    )
    gathered = exchange(packed, LAYER)
    partials, image_own, upstream = call(
        project_body,
        [((TP, 64, 256), BF16), ((ROWS, WIDE), BF16), ((LAYERS, TILE, WIDE), F32)],
        ids,
        gathered,
        kv_weight,
        other_weight,
        smem=(0,),
    )
    image_oth = swap_cores(image_own)
    (kv_own,) = call(sum_body, [((4, 64, 256), BF16)], exchange(partials, TPAX))
    kv = exchange(kv_own, QUAD)
    to_mid, probs, attn = call(
        forward_body,
        [((LAYERS, 16, WIDE), BF16), ((512, 256), F32), ((512, HD), F32)],
        ids,
        gate_logit,
        kv,
        queries,
        query_gain,
        key_gain,
        upstream,
        smem=(0, 1),
    )
    mid = exchange(to_mid, LAYER)
    to_sum, query_grad = call(
        backward_body,
        [((4, 144, HD), BF16), ((1, 2, 64, WIDE), BF16)],
        ids,
        gate_logit,
        mid,
        kv,
        queries,
        query_gain,
        key_gain,
        probs,
        attn,
        smem=(0, 1),
    )
    (to_spread,) = call(
        grad_body,
        [((TP, 144, HD), BF16)],
        ids,
        exchange(to_sum, QUAD),
        kv_own,
        key_gain,
        smem=(0,),
    )
    pieces = exchange(to_spread, TPAX)
    to_return, own_grads, oth_grads = call(
        image_body,
        [((LAYERS, 16, WIDE), BF16), ((ROWS, 1024), BF16), ((ROWS, 1024), BF16)],
        ids,
        pieces,
        kv_weight,
        other_weight,
        mid,
        smem=(0,),
        scratch=[pltpu.VMEM((ROWS, WIDE), F32)],
    )
    other_grads = swap_cores(oth_grads)
    returned = exchange(to_return, LAYER)
    (weight_grad,) = call(
        weight_body, [((1, FEAT, 1024), BF16)], image_own, image_oth, own_grads, other_grads
    )
    residual, image_grad, gates = call(
        final_body,
        [((1, 2, 64, WIDE), BF16), ((2, 4, FEAT), F32), ((1, LAYERS), F32)],
        returned,
    )
    return residual, query_grad, weight_grad, image_grad, gates.reshape(LAYERS)


def solution(mesh):
    split = Mesh(
        mesh.devices.reshape(4, 4, 2, 2, 4, 2), ("yl", "x", "core", "yh", "zh", "zl")
    )
    tokens = P(SECTION, None, None, TPAX)
    weights = P(SECTION, TPAX, None)
    image = P(None, SECTION, TPAX)
    return jax.shard_map(
        local,
        mesh=split,
        in_specs=(image, weights, tokens, P(), P(), P(), tokens),
        out_specs=(tokens, tokens, weights, image, P()),
        check_vma=False,
    )
```

```python
import math

import jax
import jax.numpy as jnp
from jax import lax
from jax.experimental import pallas as pl
from jax.experimental.pallas import tpu as pltpu
from jax.sharding import Mesh, PartitionSpec as P

F32 = jnp.float32
BF16 = jnp.bfloat16
EPS = 1e-05
HD = 128
FEAT = 480
WIDE = 512
ROWS = 128
LAYERS = 16
TP = 16
SCALE = 1.0 / math.sqrt(HD)

SECTION = ("yl", "x", "core")
LAYER = ("yl", "x")
LAYER_PAIR = ("yl", "x", "zl")
TPAX = ("yh", "zh", "zl")

NT = (((1,), (1,)), ((), ()))
TN = (((0,), (0,)), ((), ()))


def call(body, outs, *args, smem=(), held=(), far=(), scratch=(), vmem_mib=40):
    space = {i: pltpu.SMEM for i in smem} | {i: pl.ANY for i in held} | {i: pltpu.HBM for i in far}
    specs = [pl.BlockSpec(memory_space=space.get(i, pltpu.VMEM)) for i in range(len(args))]
    vmem = pl.BlockSpec(memory_space=pltpu.VMEM)
    return pl.pallas_call(
        body,
        out_shape=[jax.ShapeDtypeStruct(*o) for o in outs],
        in_specs=specs,
        out_specs=[vmem] * len(outs),
        scratch_shapes=list(scratch),
        compiler_params=pltpu.CompilerParams(vmem_limit_bytes=vmem_mib * 2**20),
    )(*args)


def dot(a, b, dims=(((1,), (0,)), ((), ()))):
    return lax.dot_general(a, b, dims, preferred_element_type=F32)


def stack_heads(x):
    return jnp.concatenate([x[:, h * HD : (h + 1) * HD] for h in range(4)], axis=0)


def unstack_heads(x, rows):
    return jnp.concatenate([x[h * rows : (h + 1) * rows] for h in range(4)], axis=1)


def pick_row(ref, layer):
    return ref[pl.ds(layer, 1), :]


def three_parts(x):
    first = x.astype(BF16).astype(F32)
    second = (x - first).astype(BF16).astype(F32)
    third = x - first - second
    lane = lax.broadcasted_iota(jnp.int32, (16, HD), 1)
    row = lax.broadcasted_iota(jnp.int32, (16, HD), 0)
    tile = jnp.where(lane == 0, first, jnp.where(lane == 1, second, jnp.where(lane == 2, third, 0.0)))
    return jnp.where(row == 0, tile, 0.0)


def swap_quads(a, b):
    low = lax.broadcasted_iota(jnp.int32, a.shape, 0) < 4
    return jnp.where(low, a, pltpu.roll(b, 4, 0)), jnp.where(low, pltpu.roll(a, 4, 0), b)


def norm(x):
    return lax.rsqrt(jnp.mean(x * x, axis=-1, keepdims=True) + EPS)


def norm_back(values, inverse, gain, upstream):
    weighted = gain * upstream
    inner = jnp.mean(values * weighted, axis=-1, keepdims=True)
    return inverse * (weighted - values * inverse * inverse * inner)


def pack_body(far_img, far_cot, out, wide, img, cot, sems):
    copies = [
        pltpu.make_async_copy(far_img, img, sems.at[0]),
        pltpu.make_async_copy(far_cot, cot, sems.at[1]),
    ]
    for copy in copies:
        copy.start()
    wide[...] = jnp.zeros((8, WIDE), F32)
    for copy in copies:
        copy.wait()
    wide[0:4, 0:FEAT] = img[0].astype(F32)
    wide[4:8, 0:FEAT] = img[1].astype(F32)
    tile = stack_heads(wide[...]).astype(BF16)
    for m in range(2):
        rows = stack_heads(cot[0, m])
        for i in range(LAYERS):
            out[i, 32 + 16 * m : 48 + 16 * m] = rows[16 * i : 16 * i + 16]
    for i in range(LAYERS):
        out[i, 0:32] = tile


def stage_body(far_own, far_oth, w_own, w_oth, sems):
    copies = [
        pltpu.make_async_copy(far_own, w_own, sems.at[0]),
        pltpu.make_async_copy(far_oth, w_oth, sems.at[1]),
    ]
    for copy in copies:
        copy.start()
    for copy in copies:
        copy.wait()


def half_body(ids, queries, out):
    out[...] = queries[0, 1 - ids[2]]


def project_body(ids, gathered, w_own, w_oth, _, partials, image, wide):
    core = ids[1]
    for pair in range(8):
        a = unstack_heads(gathered[2 * pair, 0:32].astype(F32), 8)
        b = unstack_heads(gathered[2 * pair + 1, 0:32].astype(F32), 8)
        first, second = swap_quads(a, b)
        wide[8 * pair : 8 * pair + 8] = first
        wide[64 + 8 * pair : 72 + 8 * pair] = second
    rows = wide[...].astype(BF16)
    image[...] = rows
    feats = rows[:, :FEAT]
    for which, w in ((0, w_own), (1, w_oth)):
        half = core if which == 0 else 1 - core
        sums = dot(feats, w[0]).astype(BF16)
        for k in range(4):
            for m in range(2):
                partials[8 * half + 2 * k + m] = sums[m * 64 : (m + 1) * 64, k * 256 : (k + 1) * 256]


def suffix_body(gathered, out):
    for m in range(2):
        total = jnp.zeros((16, HD), F32)
        for j in reversed(range(LAYERS)):
            total = total + gathered[j, 32 + 16 * m : 48 + 16 * m].astype(F32)
            out[j, m] = total.astype(BF16)


def sum_body(pieces, _, out):
    total = pieces[0].astype(F32)
    for t in range(1, TP):
        total = total + pieces[t].astype(F32)
    out[...] = total.astype(BF16)


def attend_body(
    ids,
    gate,
    kv_own,
    kv_oth,
    own_queries,
    pair_queries,
    query_gain,
    key_gain,
    sums,
    out,
    probs_out,
    attn_out,
    query_out,
):
    layer, zl = ids[0], ids[2]
    both = jnp.concatenate([kv_own[...], kv_oth[...]], axis=0)
    keys = both[:, :HD].astype(F32)
    key_low = (keys * norm(keys) * pick_row(key_gain, layer)).astype(BF16)
    rows = jnp.concatenate([stack_heads(own_queries[0, zl]), stack_heads(pair_queries[...])], axis=0)
    rows = rows.astype(F32)
    query_low = (rows * norm(rows) * pick_row(query_gain, layer)).astype(BF16)
    query_out[...] = rows
    scores = dot(query_low, key_low, NT) * SCALE
    expo = jnp.exp(scores - jnp.max(scores, axis=-1, keepdims=True))
    probs = expo / jnp.sum(expo, axis=-1, keepdims=True)
    probs_out[...] = probs
    attn = dot(probs.astype(BF16), both[:, HD:])
    attn_out[...] = attn
    tanh = jnp.tanh(jnp.full((1, 1), gate[layer], F32))
    branch = (tanh * attn).astype(BF16).reshape(2, LAYERS, 16, HD)
    out[:, :, 0:16] = sums[...]
    out[:, zl, 16:32] = branch[0]
    out[:, 1 - zl, 16:32] = branch[1]


def back_body(
    ids, gate, mid, kv_own, kv_oth, rows_in, query_gain, key_gain, probs_in, attn_in,
    kept, sent, own_grad, pair_grad, residual,
):
    layer, zl = ids[0], ids[2]
    both = jnp.concatenate([kv_own[...], kv_oth[...]], axis=0)
    keys = both[:, :HD].astype(F32)
    values = both[:, HD:]
    key_low = (keys * norm(keys) * pick_row(key_gain, layer)).astype(BF16)
    rows = rows_in[...]
    inverse = norm(rows)
    gain = pick_row(query_gain, layer)
    query_low = (rows * inverse * gain).astype(BF16)
    probs = probs_in[...]
    attn = attn_in[...]
    tanh = jnp.tanh(jnp.full((1, 1), gate[layer], F32))
    upstream = jnp.concatenate(
        [mid[:, zl, 0:16].reshape(256, HD), mid[:, 1 - zl, 0:16].reshape(256, HD)], axis=0
    ).astype(F32)
    d_attn = (tanh * upstream).astype(BF16)
    d_prob = dot(d_attn, values, NT)
    inner = jnp.sum(d_prob * probs, axis=-1, keepdims=True)
    d_score = (probs * (d_prob - inner) * SCALE).astype(BF16)
    d_value = dot(probs.astype(BF16), d_attn, TN)
    d_key_hat = dot(d_score, query_low, TN)
    by_row = jnp.sum(upstream * attn, axis=1, keepdims=True)
    gate_sum = (1.0 - tanh * tanh) * jnp.sum(by_row, axis=0, keepdims=True)
    extra = three_parts(gate_sum)
    kept[0:64] = d_key_hat[0:64]
    kept[64:128] = d_value[0:64]
    kept[128:144] = extra
    sent[0:64] = d_key_hat[64:128].astype(BF16)
    sent[64:128] = d_value[64:128].astype(BF16)
    sent[128:144] = extra.astype(BF16)
    d_query_hat = dot(d_score, key_low)
    grad = norm_back(rows, inverse, gain, d_query_hat)
    own_grad[...] = unstack_heads(grad[0:256], 64).astype(BF16)
    pair_grad[...] = unstack_heads(grad[256:512], 64).astype(BF16)
    for m in range(2):
        total = jnp.zeros((16, HD), F32)
        for j in range(LAYERS):
            total = total + mid[j, m, 16:32].astype(F32)
            residual[j, 16 * m : 16 * m + 16] = total.astype(BF16)


def spread_body(ids, kept, received, kv_own, key_gain, out):
    total = kept[...] + received[...].astype(F32)
    keys = kv_own[:, :HD].astype(F32)
    d_keys = norm_back(keys, norm(keys), pick_row(key_gain, ids[0]), total[0:64])
    gate_sum = jnp.sum(total[128:136], axis=1, keepdims=True)[0:1]
    tile = jnp.concatenate([d_keys, total[64:128], three_parts(gate_sum)], axis=0).astype(BF16)
    for t in range(TP):
        out[t] = tile


def columns(pieces, half):
    parts = []
    for m in range(2):
        row = []
        for k in range(4):
            tile = pieces[8 * half + 2 * k + m]
            row += [tile[0:64], tile[64:128]]
        parts.append(jnp.concatenate(row, axis=1))
    return jnp.concatenate(parts, axis=0)


def part_body(ids, pieces, _, own_grads, oth_grads):
    own_grads[...] = columns(pieces, ids[1])
    oth_grads[...] = columns(pieces, 1 - ids[1])


def image_body(ids, pieces, w_own, w_oth, residual, out, wide):
    core = ids[1]
    own = columns(pieces, core)
    oth = columns(pieces, 1 - core)
    term = (dot(w_own[0], own, NT) + dot(w_oth[0], oth, NT)).T
    gate_rows = pieces[0, 128:144].astype(F32)[0:8]
    for t in range(1, TP):
        gate_rows = gate_rows + pieces[t, 128:144].astype(F32)[0:8]
    gate_sum = jnp.sum(gate_rows, axis=1, keepdims=True)[0:1]
    wide[:, WIDE - HD :] = jnp.zeros((ROWS, HD), F32)
    wide[:, 0:FEAT] = term
    wide[:, FEAT : FEAT + 3] = jnp.broadcast_to(three_parts(gate_sum)[0:1, 0:3], (ROWS, 3))
    for pair in range(8):
        a, b = swap_quads(wide[8 * pair : 8 * pair + 8], wide[64 + 8 * pair : 72 + 8 * pair])
        out[2 * pair, 0:32] = stack_heads(a).astype(BF16)
        out[2 * pair + 1, 0:32] = stack_heads(b).astype(BF16)
    for j in range(LAYERS):
        out[j, 32:64] = residual[j]


def weight_body(image_own, image_oth, own_grads, oth_grads, out, token):
    token[...] = jnp.zeros((8, HD), F32)
    total = dot(image_own[:, :FEAT], own_grads[...], TN)
    total = total + dot(image_oth[:, :FEAT], oth_grads[...], TN)
    out[0] = total.astype(BF16)


def final_body(ids, returned, own_part, pair_part, _, residual, image, gates, query_grad):
    zl = ids[2]
    query_grad[0, zl] = own_part[...]
    query_grad[0, 1 - zl] = pair_part[...]
    total = jnp.zeros((8, WIDE), F32)
    lane = lax.broadcasted_iota(jnp.int32, (1, HD), 1)
    line = jnp.zeros((1, HD), F32)
    for i in range(LAYERS):
        both = unstack_heads(returned[i, 0:32].astype(F32), 8)
        total = total + both
        tail = jnp.sum(both[0:1, FEAT : FEAT + 3], axis=1, keepdims=True)
        line = line + jnp.where(lane == i, tail, 0.0)
    for m in range(2):
        rows = returned[:, 32 + 16 * m : 48 + 16 * m].reshape(256, HD)
        residual[0, m] = unstack_heads(rows, 64)
    image[0] = total[0:4, :FEAT]
    image[1] = total[4:8, :FEAT]
    gates[...] = line[:, :LAYERS]


def swap(x, axis):
    return lax.ppermute(x, axis, [(0, 1), (1, 0)])


def exchange(x, axes):
    return lax.all_to_all(x, axes, 0, 0)


def local(image_feats, kv_weight, queries, query_gain, key_gain, gate_logit, cotangent):
    ids = jnp.stack([lax.axis_index(LAYER), lax.axis_index("core"), lax.axis_index("zl")])
    ids = ids.astype(jnp.int32)
    (half_queries,) = call(half_body, [((64, WIDE), BF16)], ids, queries, smem=(0,))
    pair_queries = swap(half_queries, "zl")
    w_own, w_oth = call(
        stage_body,
        [((1, FEAT, 1024), BF16), ((1, FEAT, 1024), BF16)],
        kv_weight,
        swap(kv_weight, "core"),
        far=(0, 1),
        scratch=[pltpu.SemaphoreType.DMA((2,))],
    )
    (packed,) = call(
        pack_body,
        [((LAYERS, 64, HD), BF16)],
        image_feats,
        cotangent,
        far=(0, 1),
        vmem_mib=62,
        scratch=[
            pltpu.VMEM((8, WIDE), F32),
            pltpu.VMEM((2, 4, FEAT), BF16),
            pltpu.VMEM((1, 2, 64, WIDE), BF16),
            pltpu.SemaphoreType.DMA((2,)),
        ],
    )
    gathered = exchange(packed, LAYER)
    partials, image_own = call(
        project_body,
        [((TP, 64, 256), BF16), ((ROWS, WIDE), BF16)],
        ids,
        gathered,
        w_own,
        w_oth,
        pair_queries,
        smem=(0,),
        held=(4,),
        scratch=[pltpu.VMEM((ROWS, WIDE), F32)],
    )
    image_oth = swap(image_own, "core")
    pieces = exchange(partials, TPAX)
    (sums,) = call(suffix_body, [((LAYERS, 2, 16, HD), BF16)], gathered)
    (kv_own,) = call(sum_body, [((64, 256), BF16)], pieces, image_oth, held=(1,))
    kv_oth = swap(kv_own, "core")
    to_mid, probs, attn, rows = call(
        attend_body,
        [
            ((LAYERS, 2, 32, HD), BF16),
            ((512, HD), F32),
            ((512, HD), F32),
            ((512, HD), F32),
        ],
        ids,
        gate_logit,
        kv_own,
        kv_oth,
        queries,
        pair_queries,
        query_gain,
        key_gain,
        sums,
        smem=(0, 1),
    )
    mid = exchange(to_mid.reshape(2 * LAYERS, 32, HD), LAYER_PAIR).reshape(LAYERS, 2, 32, HD)
    kept, sent, own_grad, pair_grad, residuals = call(
        back_body,
        [
            ((144, HD), F32),
            ((144, HD), BF16),
            ((64, WIDE), BF16),
            ((64, WIDE), BF16),
            ((LAYERS, 32, HD), BF16),
        ],
        ids,
        gate_logit,
        mid,
        kv_own,
        kv_oth,
        rows,
        query_gain,
        key_gain,
        probs,
        attn,
        smem=(0, 1),
    )
    received = swap(sent, "core")
    (to_spread,) = call(
        spread_body, [((TP, 144, HD), BF16)], ids, kept, received, kv_own, key_gain, smem=(0,)
    )
    grad_pieces = exchange(to_spread, TPAX)
    other_part = swap(pair_grad, "zl")
    (to_return,) = call(
        image_body,
        [((LAYERS, 64, HD), BF16)],
        ids,
        grad_pieces,
        w_own,
        w_oth,
        residuals,
        smem=(0,),
        scratch=[pltpu.VMEM((ROWS, WIDE), F32)],
    )
    returned = exchange(to_return, LAYER)
    own_grads, oth_grads = call(
        part_body,
        [((ROWS, 1024), BF16), ((ROWS, 1024), BF16)],
        ids,
        grad_pieces,
        to_return,
        smem=(0,),
        held=(2,),
    )
    other_grads = swap(oth_grads, "core")
    weight_grad, token = call(
        weight_body,
        [((1, FEAT, 1024), BF16), ((8, HD), F32)],
        image_own,
        image_oth,
        own_grads,
        other_grads,
    )
    residual, image_grad, gates, query_grad = call(
        final_body,
        [
            ((1, 2, 64, WIDE), BF16),
            ((2, 4, FEAT), F32),
            ((1, LAYERS), F32),
            ((1, 2, 64, WIDE), BF16),
        ],
        ids,
        returned,
        own_grad,
        other_part,
        token,
        smem=(0,),
        held=(4,),
    )
    return residual, query_grad, weight_grad, image_grad, gates.reshape(LAYERS)


def solution(mesh):
    split = Mesh(
        mesh.devices.reshape(4, 4, 2, 2, 4, 2), ("yl", "x", "core", "yh", "zh", "zl")
    )
    tokens = P(SECTION, None, None, TPAX)
    weights = P(SECTION, TPAX, None)
    image = P(None, SECTION, TPAX)
    return jax.shard_map(
        local,
        mesh=split,
        in_specs=(image, weights, tokens, P(), P(), P(), tokens),
        out_specs=(tokens, tokens, weights, image, P()),
        check_vma=False,
    )
```

```python
import math

import jax
import jax.numpy as jnp
from jax import lax
from jax.experimental import pallas as pl
from jax.experimental.pallas import tpu as pltpu
from jax.sharding import Mesh, PartitionSpec as P

F32 = jnp.float32
BF16 = jnp.bfloat16
EPS = 1e-05
HD = 128
FEAT = 480
WIDE = 512
ROWS = 128
LAYERS = 16
TP = 16
SCALE = 1.0 / math.sqrt(HD)

SECTION = ("yl", "x", "core")
LAYER = ("yl", "x")
PLACE = ("x", "yl")
PLACE_PAIR = ("yl", "x", "tp")
TPAX = "tp"
TP_ORDER = [15, 14, 13, 12, 11, 10, 9, 8, 7, 6, 5, 4, 3, 2, 1, 0]

NT = (((1,), (1,)), ((), ()))
TN = (((0,), (0,)), ((), ()))


def call(body, outs, *args, smem=(), held=(), far=(), scratch=(), vmem_mib=40):
    space = {i: pltpu.SMEM for i in smem} | {i: pl.ANY for i in held} | {i: pltpu.HBM for i in far}
    specs = [pl.BlockSpec(memory_space=space.get(i, pltpu.VMEM)) for i in range(len(args))]
    vmem = pl.BlockSpec(memory_space=pltpu.VMEM)
    return pl.pallas_call(
        body,
        out_shape=[jax.ShapeDtypeStruct(*o) for o in outs],
        in_specs=specs,
        out_specs=[vmem] * len(outs),
        scratch_shapes=list(scratch),
        compiler_params=pltpu.CompilerParams(vmem_limit_bytes=vmem_mib * 2**20),
    )(*args)


def dot(a, b, dims=(((1,), (0,)), ((), ()))):
    return lax.dot_general(a, b, dims, preferred_element_type=F32)


def stack_heads(x):
    return jnp.concatenate([x[:, h * HD : (h + 1) * HD] for h in range(4)], axis=0)


def unstack_heads(x, rows):
    return jnp.concatenate([x[h * rows : (h + 1) * rows] for h in range(4)], axis=1)


def pick_row(ref, layer):
    return ref[pl.ds(layer, 1), :]


def three_parts(x):
    first = x.astype(BF16).astype(F32)
    second = (x - first).astype(BF16).astype(F32)
    third = x - first - second
    lane = lax.broadcasted_iota(jnp.int32, (16, HD), 1)
    row = lax.broadcasted_iota(jnp.int32, (16, HD), 0)
    tile = jnp.where(lane == 0, first, jnp.where(lane == 1, second, jnp.where(lane == 2, third, 0.0)))
    return jnp.where(row == 0, tile, 0.0)


def swap_quads(a, b):
    low = lax.broadcasted_iota(jnp.int32, a.shape, 0) < 4
    return jnp.where(low, a, pltpu.roll(b, 4, 0)), jnp.where(low, pltpu.roll(a, 4, 0), b)


def norm(x):
    return lax.rsqrt(jnp.mean(x * x, axis=-1, keepdims=True) + EPS)


def norm_back(values, inverse, gain, upstream):
    weighted = gain * upstream
    inner = jnp.mean(values * weighted, axis=-1, keepdims=True)
    return inverse * (weighted - values * inverse * inverse * inner)


def pack_body(far_img, far_cot, out, wide, img, cot, sems):
    copies = [
        pltpu.make_async_copy(far_img, img, sems.at[0]),
        pltpu.make_async_copy(far_cot, cot, sems.at[1]),
    ]
    for copy in copies:
        copy.start()
    wide[...] = jnp.zeros((8, WIDE), F32)
    for copy in copies:
        copy.wait()
    wide[0:4, 0:FEAT] = img[0].astype(F32)
    wide[4:8, 0:FEAT] = img[1].astype(F32)
    tile = stack_heads(wide[...]).astype(BF16)
    for m in range(2):
        rows = stack_heads(cot[0, m])
        for i in range(LAYERS):
            out[i, 32 + 16 * m : 48 + 16 * m] = rows[16 * i : 16 * i + 16]
    for i in range(LAYERS):
        out[i, 0:32] = tile


def stage_body(far, near, sem):
    copy = pltpu.make_async_copy(far, near, sem)
    copy.start()
    copy.wait()


def half_body(ids, queries, out):
    out[...] = queries[0, 1 - ids[2]]


def project_body(ids, gathered, w_own, w_oth, _, partials, image, wide):
    core = ids[1]
    for pair in range(8):
        a = unstack_heads(gathered[2 * pair, 0:32].astype(F32), 8)
        b = unstack_heads(gathered[2 * pair + 1, 0:32].astype(F32), 8)
        first, second = swap_quads(a, b)
        wide[8 * pair : 8 * pair + 8] = first
        wide[64 + 8 * pair : 72 + 8 * pair] = second
    rows = wide[...].astype(BF16)
    image[...] = rows
    feats = rows[:, :FEAT]
    for which, w in ((0, w_own), (1, w_oth)):
        half = core if which == 0 else 1 - core
        sums = dot(feats, w[0]).astype(BF16)
        for k in range(4):
            for m in range(2):
                partials[place_of(half, 2 * k + m)] = sums[m * 64 : (m + 1) * 64, k * 256 : (k + 1) * 256]


def suffix_body(gathered, out):
    for m in range(2):
        total = jnp.zeros((16, HD), F32)
        for j in reversed(range(LAYERS)):
            yl, x = divmod(j, 4)
            total = total + gathered[4 * x + yl, 32 + 16 * m : 48 + 16 * m].astype(F32)
            out[yl, m, x] = total.astype(BF16)


def sum_body(pieces, _, __, out):
    total = pieces[0].astype(F32)
    for t in range(1, TP):
        total = total + pieces[t].astype(F32)
    out[...] = total.astype(BF16)


def query_body(ids, own_queries, pair_queries, query_gain, rows_out, low_out):
    rows = jnp.concatenate(
        [stack_heads(own_queries[0, ids[2]]), stack_heads(pair_queries[...])], axis=0
    ).astype(F32)
    rows_out[...] = rows
    low_out[...] = (rows * norm(rows) * pick_row(query_gain, ids[0])).astype(BF16)


def attend_body(ids, gate, kv_own, kv_oth, query_low, key_gain, sums, out, probs_out, attn_out):
    layer, zl = ids[0], ids[2]
    both = jnp.concatenate([kv_own[...], kv_oth[...]], axis=0)
    keys = both[:, :HD].astype(F32)
    key_low = (keys * norm(keys) * pick_row(key_gain, layer)).astype(BF16)
    scores = dot(query_low[...], key_low, NT) * SCALE
    expo = jnp.exp(scores - jnp.max(scores, axis=-1, keepdims=True))
    probs = expo / jnp.sum(expo, axis=-1, keepdims=True)
    probs_out[...] = probs
    attn = dot(probs.astype(BF16), both[:, HD:])
    attn_out[...] = attn
    tanh = jnp.tanh(jnp.full((1, 1), gate[layer], F32))
    branch = (tanh * attn).astype(BF16).reshape(2, LAYERS, 16, HD)
    out[:, :, :, 0:16] = sums[...]
    for place in range(LAYERS):
        x, yl = divmod(place, 4)
        out[yl, zl, x, 16:32] = branch[0, place]
        out[yl, 1 - zl, x, 16:32] = branch[1, place]


def back_body(
    ids, gate, mid, kv_own, kv_oth, rows_in, low_in, query_gain, key_gain, probs_in, attn_in,
    kept, sent, own_grad, pair_grad, residual,
):
    layer, zl = ids[0], ids[2]
    both = jnp.concatenate([kv_own[...], kv_oth[...]], axis=0)
    keys = both[:, :HD].astype(F32)
    values = both[:, HD:]
    key_low = (keys * norm(keys) * pick_row(key_gain, layer)).astype(BF16)
    rows = rows_in[...]
    inverse = norm(rows)
    gain = pick_row(query_gain, layer)
    query_low = low_in[...]
    probs = probs_in[...]
    attn = attn_in[...]
    tanh = jnp.tanh(jnp.full((1, 1), gate[layer], F32))
    parts = []
    for pair in (zl, 1 - zl):
        for place in range(LAYERS):
            x, yl = divmod(place, 4)
            parts.append(mid[yl, pair, x, 0:16])
    upstream = jnp.concatenate(parts, axis=0).astype(F32)
    d_attn = (tanh * upstream).astype(BF16)
    d_prob = dot(d_attn, values, NT)
    inner = jnp.sum(d_prob * probs, axis=-1, keepdims=True)
    d_score = (probs * (d_prob - inner) * SCALE).astype(BF16)
    d_value = dot(probs.astype(BF16), d_attn, TN)
    d_key_hat = dot(d_score, query_low, TN)
    by_row = jnp.sum(upstream * attn, axis=1, keepdims=True)
    gate_sum = (1.0 - tanh * tanh) * jnp.sum(by_row, axis=0, keepdims=True)
    extra = three_parts(gate_sum)
    kept[0:64] = d_key_hat[0:64]
    kept[64:128] = d_value[0:64]
    kept[128:144] = extra
    sent[0:64] = d_key_hat[64:128].astype(BF16)
    sent[64:128] = d_value[64:128].astype(BF16)
    sent[128:144] = extra.astype(BF16)
    d_query_hat = dot(d_score, key_low)
    grad = norm_back(rows, inverse, gain, d_query_hat)
    own_grad[...] = unstack_heads(grad[0:256], 64).astype(BF16)
    pair_grad[...] = unstack_heads(grad[256:512], 64).astype(BF16)
    for m in range(2):
        total = jnp.zeros((16, HD), F32)
        for j in range(LAYERS):
            yl, x = divmod(j, 4)
            total = total + mid[yl, m, x, 16:32].astype(F32)
            residual[4 * x + yl, 16 * m : 16 * m + 16] = total.astype(BF16)


def spread_body(ids, kept, received, kv_own, key_gain, out):
    total = kept[...] + received[...].astype(F32)
    keys = kv_own[:, :HD].astype(F32)
    d_keys = norm_back(keys, norm(keys), pick_row(key_gain, ids[0]), total[0:64])
    gate_sum = jnp.sum(total[128:136], axis=1, keepdims=True)[0:1]
    tile = jnp.concatenate([d_keys, total[64:128], three_parts(gate_sum)], axis=0).astype(BF16)
    for t in range(TP):
        out[t] = tile


def place_of(half, at):
    first, second = TP_ORDER.index(at), TP_ORDER.index(8 + at)
    return first + (second - first) * half


def columns(pieces, half):
    parts = []
    for m in range(2):
        row = []
        for k in range(4):
            tile = pieces[place_of(half, 2 * k + m)]
            row += [tile[0:64], tile[64:128]]
        parts.append(jnp.concatenate(row, axis=1))
    return jnp.concatenate(parts, axis=0)


def part_body(ids, pieces, _, own_grads, oth_grads):
    own_grads[...] = columns(pieces, ids[1])
    oth_grads[...] = columns(pieces, 1 - ids[1])


def image_body(ids, pieces, w_own, w_oth, residual, out, wide):
    core = ids[1]
    own = columns(pieces, core)
    oth = columns(pieces, 1 - core)
    term = (dot(w_own[0], own, NT) + dot(w_oth[0], oth, NT)).T
    gate_rows = pieces[0, 128:144].astype(F32)[0:8]
    for t in range(1, TP):
        gate_rows = gate_rows + pieces[t, 128:144].astype(F32)[0:8]
    gate_sum = jnp.sum(gate_rows, axis=1, keepdims=True)[0:1]
    wide[:, WIDE - HD :] = jnp.zeros((ROWS, HD), F32)
    wide[:, 0:FEAT] = term
    wide[:, FEAT : FEAT + 3] = jnp.broadcast_to(three_parts(gate_sum)[0:1, 0:3], (ROWS, 3))
    for pair in range(8):
        a, b = swap_quads(wide[8 * pair : 8 * pair + 8], wide[64 + 8 * pair : 72 + 8 * pair])
        out[2 * pair, 0:32] = stack_heads(a).astype(BF16)
        out[2 * pair + 1, 0:32] = stack_heads(b).astype(BF16)
    for j in range(LAYERS):
        out[j, 32:64] = residual[j]


def weight_body(image_own, image_oth, own_grads, oth_grads, out, token):
    token[...] = jnp.zeros((8, HD), F32)
    total = dot(image_own[:, :FEAT], own_grads[...], TN)
    total = total + dot(image_oth[:, :FEAT], oth_grads[...], TN)
    out[0] = total.astype(BF16)


def final_body(ids, returned, own_part, pair_part, _, residual, image, gates, query_grad):
    query_grad[0, ids[2]] = own_part[...]
    query_grad[0, 1 - ids[2]] = pair_part[...]

    total = jnp.zeros((8, WIDE), F32)
    lane = lax.broadcasted_iota(jnp.int32, (1, HD), 1)
    line = jnp.zeros((1, HD), F32)
    for i in range(LAYERS):
        both = unstack_heads(returned[i, 0:32].astype(F32), 8)
        total = total + both
        tail = jnp.sum(both[0:1, FEAT : FEAT + 3], axis=1, keepdims=True)
        line = line + jnp.where(lane == 4 * (i % 4) + i // 4, tail, 0.0)
    for m in range(2):
        rows = returned[:, 32 + 16 * m : 48 + 16 * m].reshape(256, HD)
        residual[0, m] = unstack_heads(rows, 64)
    image[0] = total[0:4, :FEAT]
    image[1] = total[4:8, :FEAT]
    gates[...] = line[:, :LAYERS]


def swap(x, axis):
    return lax.ppermute(x, axis, [(i, i ^ 1) for i in range(lax.axis_size(axis))])


def exchange(x, axes, groups=None):
    return lax.all_to_all(x, axes, 0, 0, axis_index_groups=groups)


def pair_groups():
    return [
        [(4 * yl + x) * TP + 2 * pair + m for yl in range(4) for m in range(2) for x in range(4)]
        for pair in range(TP // 2)
    ]


def local(image_feats, kv_weight, queries, query_gain, key_gain, gate_logit, cotangent):
    ids = jnp.stack([lax.axis_index(LAYER), lax.axis_index("core"), lax.axis_index("tp") % 2])
    ids = ids.astype(jnp.int32)
    (half_queries,) = call(half_body, [((64, WIDE), BF16)], ids, queries, smem=(0,))
    pair_queries = swap(half_queries, "tp")
    w_oth = swap(kv_weight, "core")
    (w_own,) = call(
        stage_body,
        [((1, FEAT, 1024), BF16)],
        kv_weight,
        far=(0,),
        scratch=[pltpu.SemaphoreType.DMA],
    )
    (packed,) = call(
        pack_body,
        [((LAYERS, 64, HD), BF16)],
        image_feats,
        cotangent,
        far=(0, 1),
        vmem_mib=62,
        scratch=[
            pltpu.VMEM((8, WIDE), F32),
            pltpu.VMEM((2, 4, FEAT), BF16),
            pltpu.VMEM((1, 2, 64, WIDE), BF16),
            pltpu.SemaphoreType.DMA((2,)),
        ],
    )
    gathered = exchange(packed, PLACE)
    partials, image_own = call(
        project_body,
        [((TP, 64, 256), BF16), ((ROWS, WIDE), BF16)],
        ids,
        gathered,
        w_own,
        w_oth,
        pair_queries,
        smem=(0,),
        held=(4,),
        scratch=[pltpu.VMEM((ROWS, WIDE), F32)],
    )
    image_oth = swap(image_own, "core")
    pieces = exchange(partials, TPAX, [TP_ORDER])
    (sums,) = call(suffix_body, [((4, 2, 4, 16, HD), BF16)], gathered)
    rows, query_low = call(
        query_body,
        [((512, HD), F32), ((512, HD), BF16)],
        ids,
        queries,
        pair_queries,
        query_gain,
        smem=(0,),
    )
    (kv_own,) = call(
        sum_body, [((64, 256), BF16)], pieces, image_oth, query_low, held=(1, 2)
    )
    kv_oth = swap(kv_own, "core")
    to_mid, probs, attn = call(
        attend_body,
        [((4, 2, 4, 32, HD), BF16), ((512, HD), F32), ((512, HD), F32)],
        ids,
        gate_logit,
        kv_own,
        kv_oth,
        query_low,
        key_gain,
        sums,
        smem=(0, 1),
    )
    mid = exchange(to_mid.reshape(2 * LAYERS, 32, HD), PLACE_PAIR, pair_groups()).reshape(4, 2, 4, 32, HD)
    kept, sent, own_grad, pair_grad, residuals = call(
        back_body,
        [
            ((144, HD), F32),
            ((144, HD), BF16),
            ((64, WIDE), BF16),
            ((64, WIDE), BF16),
            ((LAYERS, 32, HD), BF16),
        ],
        ids,
        gate_logit,
        mid,
        kv_own,
        kv_oth,
        rows,
        query_low,
        query_gain,
        key_gain,
        probs,
        attn,
        smem=(0, 1),
    )
    received = swap(sent, "core")
    (to_spread,) = call(
        spread_body, [((TP, 144, HD), BF16)], ids, kept, received, kv_own, key_gain, smem=(0,)
    )
    grad_pieces = exchange(to_spread, TPAX, [TP_ORDER])
    other_part = swap(pair_grad, "tp")
    (to_return,) = call(
        image_body,
        [((LAYERS, 64, HD), BF16)],
        ids,
        grad_pieces,
        w_own,
        w_oth,
        residuals,
        smem=(0,),
        scratch=[pltpu.VMEM((ROWS, WIDE), F32)],
    )
    returned = exchange(to_return, PLACE)
    own_grads, oth_grads = call(
        part_body,
        [((ROWS, 1024), BF16), ((ROWS, 1024), BF16)],
        ids,
        grad_pieces,
        to_return,
        smem=(0,),
        held=(2,),
    )
    other_grads = swap(oth_grads, "core")
    weight_grad, token = call(
        weight_body,
        [((1, FEAT, 1024), BF16), ((8, HD), F32)],
        image_own,
        image_oth,
        own_grads,
        other_grads,
    )
    residual, image_grad, gates, query_grad = call(
        final_body,
        [
            ((1, 2, 64, WIDE), BF16),
            ((2, 4, FEAT), F32),
            ((1, LAYERS), F32),
            ((1, 2, 64, WIDE), BF16),
        ],
        ids,
        returned,
        own_grad,
        other_part,
        token,
        smem=(0,),
        held=(4,),
    )
    return residual, query_grad, weight_grad, image_grad, gates.reshape(LAYERS)


def solution(mesh):
    split = Mesh(
        mesh.devices.reshape(4, 4, 2, 16), ("yl", "x", "core", "tp")
    )
    tokens = P(SECTION, None, None, TPAX)
    weights = P(SECTION, TPAX, None)
    image = P(None, SECTION, TPAX)
    return jax.shard_map(
        local,
        mesh=split,
        in_specs=(image, weights, tokens, P(), P(), P(), tokens),
        out_specs=(tokens, tokens, weights, image, P()),
        check_vma=False,
    )
```

```python
import math

import jax
import jax.numpy as jnp
from jax import lax
from jax.experimental import pallas as pl
from jax.experimental.pallas import tpu as pltpu
from jax.sharding import Mesh, PartitionSpec as P

F32 = jnp.float32
BF16 = jnp.bfloat16
EPS = 1e-05
HD = 128
FEAT = 480
WIDE = 512
ROWS = 128
LAYERS = 16
TP = 16
SCALE = 1.0 / math.sqrt(HD)

SECTION = ("yl", "x", "core")
LAYER = ("yl", "x")
PLACE = ("x", "yl")
PLACE_PAIR = ("yl", "x", "tp")
TPAX = "tp"
TP_ORDER = [15, 14, 13, 12, 11, 10, 9, 8, 7, 6, 5, 4, 3, 2, 1, 0]

NT = (((1,), (1,)), ((), ()))
TN = (((0,), (0,)), ((), ()))


def call(body, outs, *args, smem=(), held=(), far=(), far_out=False, scratch=(), vmem_mib=40):
    space = {i: pltpu.SMEM for i in smem} | {i: pl.ANY for i in held} | {i: pltpu.HBM for i in far}
    specs = [pl.BlockSpec(memory_space=space.get(i, pltpu.VMEM)) for i in range(len(args))]
    place = pl.BlockSpec(memory_space=pltpu.HBM if far_out else pltpu.VMEM)
    return pl.pallas_call(
        body,
        out_shape=[jax.ShapeDtypeStruct(*o) for o in outs],
        in_specs=specs,
        out_specs=[place] * len(outs),
        scratch_shapes=list(scratch),
        compiler_params=pltpu.CompilerParams(vmem_limit_bytes=vmem_mib * 2**20),
    )(*args)


def dot(a, b, dims=(((1,), (0,)), ((), ()))):
    return lax.dot_general(a, b, dims, preferred_element_type=F32)


def stack_heads(x):
    return jnp.concatenate([x[:, h * HD : (h + 1) * HD] for h in range(4)], axis=0)


def unstack_heads(x, rows):
    return jnp.concatenate([x[h * rows : (h + 1) * rows] for h in range(4)], axis=1)


def pick_row(ref, layer):
    return ref[pl.ds(layer, 1), :]


def three_parts(x):
    first = x.astype(BF16).astype(F32)
    second = (x - first).astype(BF16).astype(F32)
    third = x - first - second
    lane = lax.broadcasted_iota(jnp.int32, (16, HD), 1)
    row = lax.broadcasted_iota(jnp.int32, (16, HD), 0)
    tile = jnp.where(lane == 0, first, jnp.where(lane == 1, second, jnp.where(lane == 2, third, 0.0)))
    return jnp.where(row == 0, tile, 0.0)


def swap_quads(a, b):
    low = lax.broadcasted_iota(jnp.int32, a.shape, 0) < 4
    return jnp.where(low, a, pltpu.roll(b, 4, 0)), jnp.where(low, pltpu.roll(a, 4, 0), b)


def norm(x):
    return lax.rsqrt(jnp.mean(x * x, axis=-1, keepdims=True) + EPS)


def norm_back(values, inverse, gain, upstream):
    weighted = gain * upstream
    inner = jnp.mean(values * weighted, axis=-1, keepdims=True)
    return inverse * (weighted - values * inverse * inverse * inner)


def pack_body(far_img, far_cot, far_out, wide, img, cot, out, sems):
    copies = [pltpu.make_async_copy(far_img, img, sems.at[0])]
    copies += [pltpu.make_async_copy(far_cot.at[0, m], cot.at[m], sems.at[1 + m]) for m in range(2)]
    for copy in copies:
        copy.start()
    wide[...] = jnp.zeros((8, WIDE), F32)
    copies[0].wait()
    wide[0:4, 0:FEAT] = img[0].astype(F32)
    wide[4:8, 0:FEAT] = img[1].astype(F32)
    tile = stack_heads(wide[...]).astype(BF16)
    copies[1].wait()
    copies[2].wait()
    sends = []
    for part in range(2):
        for i in range(8 * part, 8 * part + 8):
            out[i, 0:32] = tile
            for m in range(2):
                head, row = divmod(16 * i, 64)
                out[i, 32 + 16 * m : 48 + 16 * m] = cot[m, row : row + 16, head * HD : (head + 1) * HD]
        half = pl.ds(8 * part, 8)
        sends.append(pltpu.make_async_copy(out.at[half], far_out.at[half], sems.at[3 + part]))
        sends[-1].start()
    for send in sends:
        send.wait()


def stage_body(far, near, sem):
    copy = pltpu.make_async_copy(far, near, sem)
    copy.start()
    copy.wait()


def half_body(ids, queries, out):
    out[...] = queries[0, 1 - ids[2]]


def project_body(ids, gathered, w_own, w_oth, _, partials, image, wide):
    core = ids[1]
    for pair in range(8):
        a = unstack_heads(gathered[2 * pair, 0:32].astype(F32), 8)
        b = unstack_heads(gathered[2 * pair + 1, 0:32].astype(F32), 8)
        first, second = swap_quads(a, b)
        wide[8 * pair : 8 * pair + 8] = first
        wide[64 + 8 * pair : 72 + 8 * pair] = second
    rows = wide[...].astype(BF16)
    image[...] = rows
    feats = rows[:, :FEAT]
    for which, w in ((0, w_own), (1, w_oth)):
        half = core if which == 0 else 1 - core
        sums = dot(feats, w[0]).astype(BF16)
        for k in range(4):
            for m in range(2):
                partials[place_of(half, 2 * k + m)] = sums[m * 64 : (m + 1) * 64, k * 256 : (k + 1) * 256]


def suffix_body(gathered, out):
    for m in range(2):
        total = jnp.zeros((16, HD), F32)
        for j in reversed(range(LAYERS)):
            yl, x = divmod(j, 4)
            total = total + gathered[4 * x + yl, 32 + 16 * m : 48 + 16 * m].astype(F32)
            out[yl, m, x] = total.astype(BF16)


def sum_body(pieces, _, __, out):
    total = pieces[0].astype(F32)
    for t in range(1, TP):
        total = total + pieces[t].astype(F32)
    out[...] = total.astype(BF16)


def query_body(ids, own_queries, pair_queries, query_gain, rows_out, low_out):
    rows = jnp.concatenate(
        [stack_heads(own_queries[0, ids[2]]), stack_heads(pair_queries[...])], axis=0
    ).astype(F32)
    rows_out[...] = rows
    low_out[...] = (rows * norm(rows) * pick_row(query_gain, ids[0])).astype(BF16)


def attend_body(ids, gate, kv_own, kv_oth, query_low, key_gain, sums, out, probs_out, attn_out):
    layer, zl = ids[0], ids[2]
    both = jnp.concatenate([kv_own[...], kv_oth[...]], axis=0)
    keys = both[:, :HD].astype(F32)
    key_low = (keys * norm(keys) * pick_row(key_gain, layer)).astype(BF16)
    scores = dot(query_low[...], key_low, NT) * SCALE
    expo = jnp.exp(scores - jnp.max(scores, axis=-1, keepdims=True))
    probs = expo / jnp.sum(expo, axis=-1, keepdims=True)
    probs_out[...] = probs
    attn = dot(probs.astype(BF16), both[:, HD:])
    attn_out[...] = attn
    tanh = jnp.tanh(jnp.full((1, 1), gate[layer], F32))
    branch = (tanh * attn).astype(BF16).reshape(2, LAYERS, 16, HD)
    out[:, :, :, 0:16] = sums[...]
    for place in range(LAYERS):
        x, yl = divmod(place, 4)
        out[yl, zl, x, 16:32] = branch[0, place]
        out[yl, 1 - zl, x, 16:32] = branch[1, place]


def back_body(
    ids, gate, mid, kv_own, kv_oth, rows_in, low_in, query_gain, key_gain, probs_in, attn_in,
    kept, sent, own_grad, pair_grad, residual,
):
    layer, zl = ids[0], ids[2]
    both = jnp.concatenate([kv_own[...], kv_oth[...]], axis=0)
    keys = both[:, :HD].astype(F32)
    values = both[:, HD:]
    key_low = (keys * norm(keys) * pick_row(key_gain, layer)).astype(BF16)
    rows = rows_in[...]
    inverse = norm(rows)
    gain = pick_row(query_gain, layer)
    query_low = low_in[...]
    probs = probs_in[...]
    attn = attn_in[...]
    tanh = jnp.tanh(jnp.full((1, 1), gate[layer], F32))
    parts = []
    for pair in (zl, 1 - zl):
        for place in range(LAYERS):
            x, yl = divmod(place, 4)
            parts.append(mid[yl, pair, x, 0:16])
    upstream = jnp.concatenate(parts, axis=0).astype(F32)
    d_attn = (tanh * upstream).astype(BF16)
    d_prob = dot(d_attn, values, NT)
    inner = jnp.sum(d_prob * probs, axis=-1, keepdims=True)
    d_score = (probs * (d_prob - inner) * SCALE).astype(BF16)
    d_value = dot(probs.astype(BF16), d_attn, TN)
    d_key_hat = dot(d_score, query_low, TN)
    by_row = jnp.sum(upstream * attn, axis=1, keepdims=True)
    gate_sum = (1.0 - tanh * tanh) * jnp.sum(by_row, axis=0, keepdims=True)
    extra = three_parts(gate_sum)
    kept[0:64] = d_key_hat[0:64]
    kept[64:128] = d_value[0:64]
    kept[128:144] = extra
    sent[0:64] = d_key_hat[64:128].astype(BF16)
    sent[64:128] = d_value[64:128].astype(BF16)
    sent[128:144] = extra.astype(BF16)
    d_query_hat = dot(d_score, key_low)
    grad = norm_back(rows, inverse, gain, d_query_hat)
    own_grad[...] = unstack_heads(grad[0:256], 64).astype(BF16)
    pair_grad[...] = unstack_heads(grad[256:512], 64).astype(BF16)
    for m in range(2):
        total = jnp.zeros((16, HD), F32)
        for j in range(LAYERS):
            yl, x = divmod(j, 4)
            total = total + mid[yl, m, x, 16:32].astype(F32)
            residual[4 * x + yl, 16 * m : 16 * m + 16] = total.astype(BF16)


def spread_body(ids, kept, received, kv_own, key_gain, out):
    total = kept[...] + received[...].astype(F32)
    keys = kv_own[:, :HD].astype(F32)
    d_keys = norm_back(keys, norm(keys), pick_row(key_gain, ids[0]), total[0:64])
    gate_sum = jnp.sum(total[128:136], axis=1, keepdims=True)[0:1]
    tile = jnp.concatenate([d_keys, total[64:128], three_parts(gate_sum)], axis=0).astype(BF16)
    for t in range(TP):
        out[t] = tile


def place_of(half, at):
    first, second = TP_ORDER.index(at), TP_ORDER.index(8 + at)
    return first + (second - first) * half


def columns(pieces, half):
    parts = []
    for m in range(2):
        row = []
        for k in range(4):
            tile = pieces[place_of(half, 2 * k + m)]
            row += [tile[0:64], tile[64:128]]
        parts.append(jnp.concatenate(row, axis=1))
    return jnp.concatenate(parts, axis=0)


def part_body(ids, pieces, _, own_grads, oth_grads):
    own_grads[...] = columns(pieces, ids[1])
    oth_grads[...] = columns(pieces, 1 - ids[1])


def image_body(ids, pieces, w_own, w_oth, residual, out, wide):
    core = ids[1]
    own = columns(pieces, core)
    oth = columns(pieces, 1 - core)
    term = (dot(w_own[0], own, NT) + dot(w_oth[0], oth, NT)).T
    gate_rows = pieces[0, 128:144].astype(F32)[0:8]
    for t in range(1, TP):
        gate_rows = gate_rows + pieces[t, 128:144].astype(F32)[0:8]
    gate_sum = jnp.sum(gate_rows, axis=1, keepdims=True)[0:1]
    wide[:, WIDE - HD :] = jnp.zeros((ROWS, HD), F32)
    wide[:, 0:FEAT] = term
    wide[:, FEAT : FEAT + 3] = jnp.broadcast_to(three_parts(gate_sum)[0:1, 0:3], (ROWS, 3))
    for pair in range(8):
        a, b = swap_quads(wide[8 * pair : 8 * pair + 8], wide[64 + 8 * pair : 72 + 8 * pair])
        out[2 * pair, 0:32] = stack_heads(a).astype(BF16)
        out[2 * pair + 1, 0:32] = stack_heads(b).astype(BF16)
    for j in range(LAYERS):
        out[j, 32:64] = residual[j]


def weight_body(image_own, image_oth, own_grads, oth_grads, out, token):
    token[...] = jnp.zeros((8, HD), F32)
    total = dot(image_own[:, :FEAT], own_grads[...], TN)
    total = total + dot(image_oth[:, :FEAT], oth_grads[...], TN)
    out[0] = total.astype(BF16)


def final_body(ids, returned, own_part, pair_part, _, residual, image, gates, query_grad):
    query_grad[0, ids[2]] = own_part[...]
    query_grad[0, 1 - ids[2]] = pair_part[...]

    total = jnp.zeros((8, WIDE), F32)
    lane = lax.broadcasted_iota(jnp.int32, (1, HD), 1)
    line = jnp.zeros((1, HD), F32)
    for i in range(LAYERS):
        both = unstack_heads(returned[i, 0:32].astype(F32), 8)
        total = total + both
        tail = jnp.sum(both[0:1, FEAT : FEAT + 3], axis=1, keepdims=True)
        line = line + jnp.where(lane == 4 * (i % 4) + i // 4, tail, 0.0)
    for m in range(2):
        rows = returned[:, 32 + 16 * m : 48 + 16 * m].reshape(256, HD)
        residual[0, m] = unstack_heads(rows, 64)
    image[0] = total[0:4, :FEAT]
    image[1] = total[4:8, :FEAT]
    gates[...] = line[:, :LAYERS]


def swap(x, axis):
    return lax.ppermute(x, axis, [(i, i ^ 1) for i in range(lax.axis_size(axis))])


def exchange(x, axes, groups=None):
    return lax.all_to_all(x, axes, 0, 0, axis_index_groups=groups)


def pair_groups():
    return [
        [(4 * yl + x) * TP + 2 * pair + m for yl in range(4) for m in range(2) for x in range(4)]
        for pair in range(TP // 2)
    ]


def local(image_feats, kv_weight, queries, query_gain, key_gain, gate_logit, cotangent):
    ids = jnp.stack([lax.axis_index(LAYER), lax.axis_index("core"), lax.axis_index("tp") % 2])
    ids = ids.astype(jnp.int32)
    (half_queries,) = call(half_body, [((64, WIDE), BF16)], ids, queries, smem=(0,))
    pair_queries = swap(half_queries, "tp")
    w_oth = swap(kv_weight, "core")
    (w_own,) = call(
        stage_body,
        [((1, FEAT, 1024), BF16)],
        kv_weight,
        far=(0,),
        scratch=[pltpu.SemaphoreType.DMA],
    )
    (packed,) = call(
        pack_body,
        [((LAYERS, 64, HD), BF16)],
        image_feats,
        cotangent,
        far=(0, 1),
        far_out=True,
        vmem_mib=62,
        scratch=[
            pltpu.VMEM((8, WIDE), F32),
            pltpu.VMEM((2, 4, FEAT), BF16),
            pltpu.VMEM((2, 64, WIDE), BF16),
            pltpu.VMEM((LAYERS, 64, HD), BF16),
            pltpu.SemaphoreType.DMA((5,)),
        ],
    )
    gathered = exchange(packed, PLACE)
    partials, image_own = call(
        project_body,
        [((TP, 64, 256), BF16), ((ROWS, WIDE), BF16)],
        ids,
        gathered,
        w_own,
        w_oth,
        pair_queries,
        smem=(0,),
        held=(4,),
        scratch=[pltpu.VMEM((ROWS, WIDE), F32)],
    )
    image_oth = swap(image_own, "core")
    pieces = exchange(partials, TPAX, [TP_ORDER])
    (sums,) = call(suffix_body, [((4, 2, 4, 16, HD), BF16)], gathered)
    rows, query_low = call(
        query_body,
        [((512, HD), F32), ((512, HD), BF16)],
        ids,
        queries,
        pair_queries,
        query_gain,
        smem=(0,),
    )
    (kv_own,) = call(
        sum_body, [((64, 256), BF16)], pieces, image_oth, query_low, held=(1, 2)
    )
    kv_oth = swap(kv_own, "core")
    to_mid, probs, attn = call(
        attend_body,
        [((4, 2, 4, 32, HD), BF16), ((512, HD), F32), ((512, HD), F32)],
        ids,
        gate_logit,
        kv_own,
        kv_oth,
        query_low,
        key_gain,
        sums,
        smem=(0, 1),
    )
    mid = exchange(to_mid.reshape(2 * LAYERS, 32, HD), PLACE_PAIR, pair_groups()).reshape(4, 2, 4, 32, HD)
    kept, sent, own_grad, pair_grad, residuals = call(
        back_body,
        [
            ((144, HD), F32),
            ((144, HD), BF16),
            ((64, WIDE), BF16),
            ((64, WIDE), BF16),
            ((LAYERS, 32, HD), BF16),
        ],
        ids,
        gate_logit,
        mid,
        kv_own,
        kv_oth,
        rows,
        query_low,
        query_gain,
        key_gain,
        probs,
        attn,
        smem=(0, 1),
    )
    received = swap(sent, "core")
    (to_spread,) = call(
        spread_body, [((TP, 144, HD), BF16)], ids, kept, received, kv_own, key_gain, smem=(0,)
    )
    grad_pieces = exchange(to_spread, TPAX, [TP_ORDER])
    other_part = swap(pair_grad, "tp")
    (to_return,) = call(
        image_body,
        [((LAYERS, 64, HD), BF16)],
        ids,
        grad_pieces,
        w_own,
        w_oth,
        residuals,
        smem=(0,),
        scratch=[pltpu.VMEM((ROWS, WIDE), F32)],
    )
    returned = exchange(to_return, PLACE)
    own_grads, oth_grads = call(
        part_body,
        [((ROWS, 1024), BF16), ((ROWS, 1024), BF16)],
        ids,
        grad_pieces,
        to_return,
        smem=(0,),
        held=(2,),
    )
    other_grads = swap(oth_grads, "core")
    weight_grad, token = call(
        weight_body,
        [((1, FEAT, 1024), BF16), ((8, HD), F32)],
        image_own,
        image_oth,
        own_grads,
        other_grads,
    )
    residual, image_grad, gates, query_grad = call(
        final_body,
        [
            ((1, 2, 64, WIDE), BF16),
            ((2, 4, FEAT), F32),
            ((1, LAYERS), F32),
            ((1, 2, 64, WIDE), BF16),
        ],
        ids,
        returned,
        own_grad,
        other_part,
        token,
        smem=(0,),
        held=(4,),
    )
    return residual, query_grad, weight_grad, image_grad, gates.reshape(LAYERS)


def solution(mesh):
    split = Mesh(
        mesh.devices.reshape(4, 4, 2, 16), ("yl", "x", "core", "tp")
    )
    tokens = P(SECTION, None, None, TPAX)
    weights = P(SECTION, TPAX, None)
    image = P(None, SECTION, TPAX)
    return jax.shard_map(
        local,
        mesh=split,
        in_specs=(image, weights, tokens, P(), P(), P(), tokens),
        out_specs=(tokens, tokens, weights, image, P()),
        check_vma=False,
    )
```
